256 devices in a mesh: gx: 4 (over z_hi), gy: 64 (over y, z_lo, x, core).
Axes of the slice: x: 4, y: 4, z: 8 (z_hi: 4, z_lo: 2; z = z_hi * 2 + z_lo), core: 2. Of those that a mesh axis runs over, the one named last changes fastest.
Arguments:
- tokens: bfloat16 [1024, 16384], P(None, ('gx', 'gy')), may hold values from -6 to 6
- gate_weight: bfloat16 [16384, 32768], P('gx', 'gy'), may hold values from -0.046875 to 0.046875
- up_weight: bfloat16 [16384, 32768], P('gx', 'gy'), may hold values from -0.046875 to 0.046875
- down_weight: bfloat16 [32768, 16384], P('gy', 'gx'), may hold values from -0.03125 to 0.03125
Outputs:
- mixed: bfloat16 [1024, 16384], P('gy', 'gx')
The draws below stay inside these ranges and needn't reach their ends.
All inputs are finite; a program needn't handle non-finite values.
Results may differ from the reference program's by a relative error of at most 0.0049.
Values may be sent and summed in bfloat16 or wider, within the bound.
A program may use at most 128 MiB of HBM per device.

```python
import jax
import jax.numpy as jnp

D = 16384
FF = 32768
TOKENS = 1024


def level_of(own_key, dims, shards, least, largest):
    def one(axis_at, blocks):
        draws = jax.random.uniform(jax.random.fold_in(jax.random.fold_in(own_key, 6), axis_at), (blocks,), jnp.float32, least / len(shards), largest / len(shards))
        return jnp.repeat(jnp.exp(draws), dims[axis_at] // blocks).reshape((-1,) + (1,) * (len(dims) - axis_at - 1))

    factor_of = one(*shards[0])
    for cut in shards[1:]:
        factor_of = factor_of * one(*cut)
    return factor_of


def gaussian(rng, dims, width, most, split=(), kind=jnp.bfloat16):
    values = jax.random.normal(rng, dims, jnp.float32) * width
    if len(split) > 0:
        values = level_of(rng, dims, split, -0.22, 0.18) * values
    return jnp.clip(values, min=-most, max=most).astype(kind)


def setup_inputs(seed: int = 0) -> dict:
    splits = jax.random.split(jax.random.key(seed), 5)
    return {
        "tokens": gaussian(splits[0], (TOKENS, D), 1.0, 6.0, ((1, 256),)),
        "gate_weight": gaussian(splits[1], (D, FF), D ** -0.5, 0.046875, ((0, 4), (1, 64))),
        "up_weight": gaussian(splits[2], (D, FF), D ** -0.5, 0.046875, ((0, 4), (1, 64))),
        "down_weight": gaussian(splits[3], (FF, D), FF ** -0.5, 0.03125, ((0, 64), (1, 4))),
    }


def reference(tokens, gate_weight, up_weight, down_weight):
    gate = jnp.dot(tokens, gate_weight, preferred_element_type=jnp.float32)
    up = jnp.dot(tokens, up_weight, preferred_element_type=jnp.float32)
    hidden = (jax.nn.silu(gate) * up).astype(jnp.bfloat16)
    return jnp.dot(hidden, down_weight, preferred_element_type=jnp.float32).astype(jnp.bfloat16)
```

```python
import functools

import jax
import jax.numpy as jnp
from jax import lax
from jax.experimental import pallas as pl
from jax.experimental.pallas import tpu as pltpu
from jax.sharding import PartitionSpec as P

MESH = pl.DeviceIdType.MESH
F32, BF16 = jnp.float32, jnp.bfloat16
BLOCKS = 4
RING_TOKENS = False
RING_MIXED = False
MAX_SEMS = 320


def schedule(chain, gap):
    order = []
    for slot in range(len(chain) + gap * (BLOCKS - 1)):
        for b in range(BLOCKS):
            at = slot - gap * b
            if 0 <= at < len(chain):
                order.append((chain[at], b))
    return order


def kernel(
    tok_ref, wg_hbm, wu_hbm, wd_hbm, out_ref,
    wg, wu, wd, twin, twin_in, feats, part, zs, zr, hid, xs, xr, mix,
    as1, ar1, bs1, br1, aq, bq, as2, ar2, bs2, br2, res, pair_in, fin, fin_in,
    load_sem, send_sem, recv_sem,
):
    k, j = lax.axis_index("gx"), lax.axis_index("gy")
    c, x, l, y = j % 2, (j // 2) % 4, (j // 8) % 2, j // 16

    def gy(y, l, x, c):
        return ((y * 2 + l) * 4 + x) * 2 + c

    def at_x(d):
        return (k, gy(y, l, (x + d) % 4, c))

    def at_y(d):
        return (k, gy((y + d) % 4, l, x, c))

    def at_k(d):
        return ((k + d) % 4, j)

    sibling = (k, gy(y, l, x, 1 - c))
    partner = (k, gy(y, 1 - l, x, c))
    where = {"x": at_x, "y": at_y, "k": at_k}
    mine = {"x": x, "y": y, "k": k}

    loads = []
    for n, (src, dst) in enumerate(((wg_hbm, wg), (wu_hbm, wu), (wd_hbm, wd))):
        copy = pltpu.make_async_copy(src, dst, load_sem.at[n])
        copy.start()
        loads.append(copy)

    barrier = pltpu.get_barrier_semaphore()
    peers = [sibling, partner]
    peers += [at(d) for at in (at_x, at_y) for d in (1, 3, 2)]
    peers += [at_k(1), at_k(3)]
    for peer in peers:
        pl.semaphore_signal(barrier, inc=1, device_id=peer, device_id_type=MESH)

    sent = []

    def send(src, dst, to):
        n = len(sent)
        copy = pltpu.make_async_remote_copy(
            src_ref=src, dst_ref=dst, send_sem=send_sem.at[n], recv_sem=recv_sem.at[n],
            device_id=to, device_id_type=MESH,
        )
        copy.start()
        sent.append(copy)
        return copy

    for b in range(BLOCKS):
        for row in range(4):
            for col in range(4):
                first = row * 256 + (b % 2) * 128 + col * 32 + (b // 2) * 16
                v = tok_ref[first : first + 16, :]
                twin[b, row // 2, row % 2, col * 16 : col * 16 + 16, :] = jnp.concatenate([v, v], axis=1)

    pl.semaphore_wait(barrier, len(peers))
    first_swap = send(twin.at[:, 1 - c], twin_in, sibling)
    state = {}

    def ring_gather(key, axis, own, part_of, ring):
        m, at = mine[axis], where[axis]

        def start():
            s = own(m)
            state[key] = [send(s, s, at(1)), send(s, s, at(3))]
            if not ring:
                state[key].append(send(s, s, at(2)))

        def forward():
            left, right = state[key]
            left.wait_recv()
            s = part_of((m + 3) % 4, 0)
            on = [send(s, s, at(1))]
            right.wait_recv()
            s = part_of((m + 1) % 4, 1)
            on.append(send(s, s, at(3)))
            state[key] = on

        def done():
            for copy in state[key]:
                copy.wait_recv()

        return start, forward, done

    def scatter(key, axis, read, st, rc, ring):
        m, at = mine[axis], where[axis]

        def put(n, value):
            st[n] = value.astype(BF16)

        def start():
            opp, nxt, prv = (m + 2) % 4, (m + 1) % 4, (m + 3) % 4
            put(0, read(opp, 0))
            put(1, read(opp, 1))
            if ring:
                first = [send(st.at[0], rc.at[0], at(1)), send(st.at[1], rc.at[1], at(3))]
                put(2, read(nxt, 1))
                put(3, read(prv, 0))
                rest = [send(st.at[2], rc.at[2], at(1)), send(st.at[3], rc.at[3], at(3))]
                state[key] = (first, rest)
            else:
                rest = [send(st.at[pl.ds(0, 2)], rc.at[pl.ds(0, 2)], at(2))]
                for n, chunk, d in ((2, nxt, 1), (4, prv, 3)):
                    put(n, read(chunk, 0))
                    put(n + 1, read(chunk, 1))
                    rest.append(send(st.at[pl.ds(n, 2)], rc.at[pl.ds(n, 2)], at(d)))
                state[key] = ((), rest)

        def forward():
            first, rest = state[key]
            first[0].wait_recv()
            put(4, read((m + 1) % 4, 0) + rc[0].astype(F32))
            rest.append(send(st.at[4], rc.at[4], at(1)))
            first[1].wait_recv()
            put(5, read((m + 3) % 4, 1) + rc[1].astype(F32))
            rest.append(send(st.at[5], rc.at[5], at(3)))

        def done():
            for copy in state[key][1]:
                copy.wait_recv()

        def total(h):
            if ring:
                terms = (3, 4) if h == 0 else (2, 5)
            else:
                terms = (h, 2 + h, 4 + h)
            value = read(m, h)
            for n in terms:
                value = value + rc[n].astype(F32)
            return value

        return start, forward, done, total

    steps = {}

    def step(name):
        def add(f):
            steps[name] = f
            return f

        return add

    @step("pair")
    def _(b):
        if b == 0:
            first_swap.wait_recv()
        own = twin[b, c].reshape(128, 128)
        other = twin_in[b].reshape(128, 128)
        lane = lax.broadcasted_iota(jnp.int32, (128, 128), 1)
        low = jnp.where(lane < 64, 0, 1) == c
        block = jnp.where(low, own.astype(F32), other.astype(F32)).astype(BF16)
        feats[y, l, x, b, c] = block.reshape(2, 64, 128)
        s = feats.at[y, l, x, b, c]
        state["pair", b] = send(s, s, partner)

    def gathers(b):
        near = [
            ring_gather(("nx", b), "x", lambda m: feats.at[y, :, m, b, c, 0],
                        lambda m, h: feats.at[y, h, m, b, c, 0], RING_TOKENS),
            ring_gather(("ny", b), "y", lambda m: feats.at[m, :, x, b, c, 1],
                        lambda m, h: feats.at[m, h, x, b, c, 1], RING_TOKENS),
        ]
        far = [
            ring_gather(("fy", b), "y", lambda m: feats.at[m, :, :, b, c, 0],
                        lambda m, h: feats.at[m, h, :, b, c, 0], RING_TOKENS),
            ring_gather(("fx", b), "x", lambda m: feats.at[:, :, m, b, c, 1],
                        lambda m, h: feats.at[:, h, m, b, c, 1], RING_TOKENS),
        ]
        return near, far

    def to_sibling(b, d, which):
        s = feats.at[(y + d) % 4, :, :, b, c, 0] if which == 0 else feats.at[:, :, (x + d) % 4, b, c, 1]
        state.setdefault(("sib", b), []).append(send(s, s, sibling))

    @step("near")
    def _(b):
        state["pair", b].wait_recv()
        for g in gathers(b)[0]:
            g[0]()

    if RING_TOKENS:

        @step("near on")
        def _(b):
            for g in gathers(b)[0]:
                g[1]()

    @step("far")
    def _(b):
        near, far = gathers(b)
        for n in range(2):
            near[n][2]()
            far[n][0]()
        for n in range(2):
            to_sibling(b, 0, n)

    if RING_TOKENS:

        @step("far on")
        def _(b):
            for n, g in enumerate(gathers(b)[1]):
                g[1]()
                to_sibling(b, 1, n)
                to_sibling(b, 3, n)

        @step("far end")
        def _(b):
            for n, g in enumerate(gathers(b)[1]):
                g[2]()
                to_sibling(b, 2, n)
    else:

        @step("far end")
        def _(b):
            for n, d in enumerate((3, 1, 2)):
                for which, key in enumerate(("fy", "fx")):
                    state[key, b][n].wait_recv()
                    to_sibling(b, d, which)

    def z_read(b):
        return lambda chunk, h: part[b % 2, chunk, h * 32 : h * 32 + 32, :]

    @step("up")
    def _(b):
        for copy in state["sib", b]:
            copy.wait_recv()
        if b == 0:
            loads[0].wait()
            loads[1].wait()
        for which, w in enumerate((wg, wu)):

            @pl.loop(0, 2)
            def _(n):
                lhs = jnp.concatenate(
                    [feats[s // 8, s // 4 % 2, s % 4, b].reshape(256, 128) for s in range(32)], axis=1
                )
                cols = pl.ds(pl.multiple_of(n * 256, 256), 256)
                got = jnp.dot(lhs, w[:, cols], preferred_element_type=F32)
                at = pl.ds(pl.multiple_of(which * 512 + n * 256, 256), 256)
                part[b % 2, :, :, at] = got.reshape(4, 64, 256)

        state["z", b] = scatter(("zs", b), "k", z_read(b), zs.at[b], zr.at[b], True)
        state["z", b][0]()

    @step("z on")
    def _(b):
        state["z", b][1]()

    def h_gather(b):
        return ring_gather(("h", b), "k", lambda m: hid.at[b, m], lambda m, h: hid.at[b, m, pl.ds(h * 32, 32)], True)

    @step("act")
    def _(b):
        _, _, done, total = state["z", b]
        done()
        for h in range(2):
            both = total(h)
            gate, up = both[:, :512], both[:, 512:]
            value = gate / (1.0 + jnp.exp(-gate)) * up
            hid[b, k, h * 32 : h * 32 + 32, :] = value.astype(BF16)
        h_gather(b)[0]()

    @step("h on")
    def _(b):
        h_gather(b)[1]()

    @step("down")
    def _(b):
        h_gather(b)[2]()
        if b == 0:
            loads[2].wait()

        def tile(half, n):
            cols = pl.ds(pl.multiple_of(half * 2048 + n * 512, 512), 512)
            got = jnp.dot(hid[b].reshape(256, 512), wd[:, cols], preferred_element_type=F32)
            return got.reshape(4, 4, 16, 512)

        @pl.loop(0, 4)
        def _(n):
            xs[b, :, :, :, pl.ds(pl.multiple_of(n * 512, 512), 512)] = tile(1 - c, n).astype(BF16)

        state["swap", b] = send(xs.at[b], xr.at[b], sibling)

        @pl.loop(0, 4)
        def _(n):
            mix[b, :, :, :, pl.ds(pl.multiple_of(n * 512, 512), 512)] = tile(c, n)

    @step("mix")
    def _(b):
        state["swap", b].wait_recv()

        @pl.loop(0, 4)
        def _(n):
            mix[b, n] = mix[b, n] + xr[b, n].astype(F32)

        a = scatter(("a1", b), "y", lambda ch, h: mix[b, ch, 2 * h : 2 * h + 2, :, :1024],
                    as1.at[b], ar1.at[b], RING_MIXED)
        v = scatter(("b1", b), "x", lambda ch, h: mix[b, 2 * h : 2 * h + 2, ch, :, 1024:],
                    bs1.at[b], br1.at[b], RING_MIXED)
        state["m1", b] = (a, v)
        a[0]()
        v[0]()

    if RING_MIXED:

        @step("mix on")
        def _(b):
            for s in state["m1", b]:
                s[1]()

    @step("mix end")
    def _(b):
        for (_, _, done, total), q in zip(state["m1", b], (aq, bq)):
            done()
            for h in range(2):
                q[b, 2 * h : 2 * h + 2] = total(h)
        a = scatter(("a2", b), "x", lambda ch, h: aq[b, ch, :, h * 512 : h * 512 + 512],
                    as2.at[b], ar2.at[b], RING_MIXED)
        v = scatter(("b2", b), "y", lambda ch, h: bq[b, ch, :, h * 512 : h * 512 + 512],
                    bs2.at[b], br2.at[b], RING_MIXED)
        state["m2", b] = (a, v)
        a[0]()
        v[0]()

    if RING_MIXED:

        @step("rest on")
        def _(b):
            for s in state["m2", b]:
                s[1]()

    @step("rest end")
    def _(b):
        for n, (_, _, done, total) in enumerate(state["m2", b]):
            done()
            for h in range(2):
                res[b, :, n * 1024 + h * 512 : n * 1024 + h * 512 + 512] = total(h)
        if b % 2 == 1:
            p = b // 2
            state["low", p] = send(res.at[2 * p + (1 - l)], pair_in.at[p], partner)

    @step("low")
    def _(b):
        if b % 2 == 1:
            p = b // 2
            state["low", p].wait_recv()
            fin[p] = (res[2 * p + l] + pair_in[p]).astype(BF16)

    for name, b in schedule(list(steps), 2):
        steps[name](b)

    last = send(fin.at[1 - c], fin_in, sibling)
    out_ref[:, pl.ds(pl.multiple_of(c * 2048, 2048), 2048)] = fin[c]
    last.wait_recv()
    out_ref[:, pl.ds(pl.multiple_of((1 - c) * 2048, 2048), 2048)] = fin_in[...]
    for copy in sent:
        copy.wait_send()
    assert len(sent) <= MAX_SEMS


def local(tokens, gate_weight, up_weight, down_weight):
    n = BLOCKS
    scratch = [
        pltpu.VMEM((4096, 512), BF16),
        pltpu.VMEM((4096, 512), BF16),
        pltpu.VMEM((512, 4096), BF16),
        pltpu.VMEM((n, 2, 2, 64, 128), BF16),
        pltpu.VMEM((n, 2, 64, 128), BF16),
        pltpu.VMEM((4, 2, 4, n, 2, 2, 64, 128), BF16),
        pltpu.VMEM((2, 4, 64, 1024), F32),
        pltpu.VMEM((n, 6, 32, 1024), BF16),
        pltpu.VMEM((n, 6, 32, 1024), BF16),
        pltpu.VMEM((n, 4, 64, 512), BF16),
        pltpu.VMEM((n, 4, 4, 16, 2048), BF16),
        pltpu.VMEM((n, 4, 4, 16, 2048), BF16),
        pltpu.VMEM((n, 4, 4, 16, 2048), F32),
        *[pltpu.VMEM((n, 6, 2, 16, 1024), BF16) for _ in range(4)],
        *[pltpu.VMEM((n, 4, 16, 1024), F32) for _ in range(2)],
        *[pltpu.VMEM((n, 6, 16, 512), BF16) for _ in range(4)],
        pltpu.VMEM((n, 16, 2048), F32),
        pltpu.VMEM((2, 16, 2048), F32),
        pltpu.VMEM((2, 16, 2048), BF16),
        pltpu.VMEM((16, 2048), BF16),
        pltpu.SemaphoreType.DMA((3,)),
        pltpu.SemaphoreType.DMA((MAX_SEMS,)),
        pltpu.SemaphoreType.DMA((MAX_SEMS,)),
    ]
    return pl.pallas_call(
        kernel,
        name="swiglu_layer",
        out_shape=jax.ShapeDtypeStruct((16, 4096), BF16),
        in_specs=[pl.BlockSpec(memory_space=pltpu.VMEM)] + [pl.BlockSpec(memory_space=pl.ANY)] * 3,
        out_specs=pl.BlockSpec(memory_space=pltpu.VMEM),
        scratch_shapes=scratch,
        cost_estimate=pl.CostEstimate(flops=12_900_000_000, bytes_accessed=13_000_000, transcendentals=131072),
        compiler_params=pltpu.CompilerParams(
            collective_id=0, has_side_effects=True, vmem_limit_bytes=62 * 2**20
        ),
    )(tokens, gate_weight, up_weight, down_weight)


def solution(mesh):
    placed = (P(None, ("gx", "gy")), P("gx", "gy"), P("gx", "gy"), P("gy", "gx"))
    return jax.shard_map(local, mesh=mesh, in_specs=placed, out_specs=P("gy", "gx"), check_vma=False)
```

```python
import functools

import jax
import jax.numpy as jnp
from jax import lax
from jax.experimental import pallas as pl
from jax.experimental.pallas import tpu as pltpu
from jax.sharding import PartitionSpec as P

MESH = pl.DeviceIdType.MESH
F32, BF16 = jnp.float32, jnp.bfloat16
BLOCKS = 4
UNITS = 8
PER = UNITS // BLOCKS
ROWS = 1024 // UNITS
QUARTER = ROWS // 4
REST = F32
MAX_SEMS = 384

ORDER = (
    (0, 0), (0, 4), (0, 3), (0, 1), (0, 7), (1, 0), (1, 3), (1, 1), (1, 4), (2, 0), (2, 1), (0, 6),
    (2, 4), (0, 2), (1, 6), (3, 0), (4, 0), (2, 3), (1, 7), (1, 2), (3, 1), (4, 1), (5, 0), (5, 1),
    (3, 4), (3, 3), (2, 6), (6, 0), (4, 3), (2, 2), (0, 5), (6, 1), (5, 3), (7, 0), (1, 5), (3, 6),
    (7, 1), (3, 2), (4, 2), (4, 6), (6, 3), (4, 4), (2, 7), (5, 2), (5, 4), (3, 7), (2, 5), (6, 2),
    (4, 7), (8, 1), (8, 0), (5, 6), (3, 5), (4, 5), (7, 2), (7, 3), (9, 1), (5, 5), (9, 0), (6, 4),
    (8, 2), (10, 1), (8, 3), (6, 5), (5, 7), (10, 0), (7, 4), (9, 3), (9, 2), (7, 5), (6, 7), (10, 3),
    (11, 1), (6, 6), (8, 4), (10, 2), (8, 5), (7, 7), (11, 0), (7, 6), (9, 5), (11, 3), (8, 7), (9, 4),
    (8, 6), (10, 5), (10, 4), (9, 7), (9, 6), (10, 7), (10, 6), (11, 5), (11, 2), (11, 4), (12, 0), (12, 3),
    (12, 1), (11, 7), (11, 6), (12, 2), (13, 0), (12, 5), (12, 4), (12, 7), (12, 6), (13, 3), (13, 1), (14, 1),
    (13, 2), (14, 0),
)

def kernel(
    tok_ref, wg_hbm, wu_hbm, wd_hbm, out_ref,
    wg, wu, wd, twin, twin_in, feats, part, zs, zr, hid, xs, xr, mix,
    s1, r1, q1, s2, r2, res, pair_in, fin, fin_in,
    load_sem, send_sem, recv_sem,
):
    k, j = lax.axis_index("gx"), lax.axis_index("gy")
    c, x, l, y = j % 2, (j // 2) % 4, (j // 8) % 2, j // 16

    def gy(y, l, x, c):
        return ((y * 2 + l) * 4 + x) * 2 + c

    def at_x(d):
        return (k, gy(y, l, (x + d) % 4, c))

    def at_y(d):
        return (k, gy((y + d) % 4, l, x, c))

    def at_k(d):
        return ((k + d) % 4, j)

    sibling = (k, gy(y, l, x, 1 - c))
    partner = (k, gy(y, 1 - l, x, c))
    where = {"x": at_x, "y": at_y, "k": at_k}
    mine = {"x": x, "y": y, "k": k}

    loads = []
    for n, (src, dst) in enumerate(((wg_hbm, wg), (wu_hbm, wu), (wd_hbm, wd))):
        copy = pltpu.make_async_copy(src, dst, load_sem.at[n])
        copy.start()
        loads.append(copy)

    barrier = pltpu.get_barrier_semaphore()
    peers = [sibling, partner]
    peers += [at(d) for at in (at_x, at_y) for d in (1, 3, 2)]
    peers += [at_k(1), at_k(3)]
    for peer in peers:
        pl.semaphore_signal(barrier, inc=1, device_id=peer, device_id_type=MESH)

    sent = []

    def send(src, dst, to):
        n = len(sent)
        copy = pltpu.make_async_remote_copy(
            src_ref=src, dst_ref=dst, send_sem=send_sem.at[n], recv_sem=recv_sem.at[n],
            device_id=to, device_id_type=MESH,
        )
        copy.start()
        sent.append(copy)
        return copy

    for b in range(BLOCKS):
        for group in range(16):
            first = group // 4 * 256 + (b % 2) * 128 + group % 4 * 32 + (b // 2) * 16
            v = tok_ref[first : first + 16, :]
            at = b * 256 + group * 16
            u, row = at // ROWS, at % ROWS
            twin[u, row // (2 * QUARTER), row % (2 * QUARTER) : row % (2 * QUARTER) + 16, :] = jnp.concatenate(
                [v, v], axis=1
            )

    pl.semaphore_wait(barrier, len(peers))
    first_swap = send(twin.at[:, 1 - c], twin_in, sibling)
    state = {}

    def gather(key, axis, own):
        at = where[axis]

        def start():
            s = own(mine[axis])
            state[key] = [send(s, s, at(1)), send(s, s, at(3)), send(s, s, at(2))]

        def done():
            once(state[key])

        return start, done

    def ring_gather(key, own, part_of):
        def start():
            s = own(k)
            state[key] = [send(s, s, at_k(1)), send(s, s, at_k(3))]

        def forward():
            left, right = state[key]
            left.wait_recv()
            s = part_of((k + 3) % 4, 0)
            on = [send(s, s, at_k(1))]
            right.wait_recv()
            s = part_of((k + 1) % 4, 1)
            on.append(send(s, s, at_k(3)))
            state[key] = on

        return start, forward

    def scatter(key, axis, read, st, rc):
        m, at = mine[axis], where[axis]

        def start():
            copies = []
            for n, d in enumerate((2, 1, 3)):
                st[n] = read((m + d) % 4).astype(st.dtype)
                copies.append(send(st.at[n], rc.at[n], at(d)))
            state[key] = copies

        def done():
            value = read(m)
            for n in (1, 2, 0):
                state[key][n].wait_recv()
                value = value + rc[n].astype(F32)
            return value

        return start, done

    def ring_scatter(key, read, st, rc):
        def put(n, value):
            st[n] = value.astype(BF16)

        def start():
            opp, nxt, prv = (k + 2) % 4, (k + 1) % 4, (k + 3) % 4
            put(0, read(opp, 0))
            put(1, read(opp, 1))
            first = [send(st.at[0], rc.at[0], at_k(1)), send(st.at[1], rc.at[1], at_k(3))]
            put(2, read(nxt, 1))
            put(3, read(prv, 0))
            rest = [send(st.at[2], rc.at[2], at_k(1)), send(st.at[3], rc.at[3], at_k(3))]
            state[key] = (first, rest)

        def forward():
            first, rest = state[key]
            first[0].wait_recv()
            put(4, read((k + 1) % 4, 0) + rc[0].astype(F32))
            rest.append(send(st.at[4], rc.at[4], at_k(1)))
            first[1].wait_recv()
            put(5, read((k + 3) % 4, 1) + rc[1].astype(F32))
            rest.append(send(st.at[5], rc.at[5], at_k(3)))

        def done():
            once(state[key][1])

        def total(h):
            value = read(k, h)
            for n in (3, 4) if h == 0 else (2, 5):
                value = value + rc[n].astype(F32)
            return value

        return start, forward, done, total

    def once(copies):
        for copy in copies:
            copy.wait_recv()
        copies.clear()

    swap_in, weights_in, down_in = [first_swap], loads[:2], loads[2:]

    def pair(u):
        once(swap_in)
        own, other = twin[u, c], twin_in[u]
        lane = lax.broadcasted_iota(jnp.int32, own.shape, 1)
        low = jnp.where(lane < 64, 0, 1) == c
        block = jnp.where(low, own.astype(F32), other.astype(F32)).astype(BF16)
        feats[y, l, x, u, c] = block.reshape(2, QUARTER, 128)
        s = feats.at[y, l, x, u, c]
        state["pair", u] = send(s, s, partner)

    def gathers(u):
        near = [
            gather(("nx", u), "x", lambda m: feats.at[y, :, m, u, c, 0]),
            gather(("ny", u), "y", lambda m: feats.at[m, :, x, u, c, 1]),
        ]
        far = [
            gather(("fy", u), "y", lambda m: feats.at[m, :, :, u, c, 0]),
            gather(("fx", u), "x", lambda m: feats.at[:, :, m, u, c, 1]),
        ]
        return near, far

    def to_sibling(u, d, which):
        s = feats.at[(y + d) % 4, :, :, u, c, 0] if which == 0 else feats.at[:, :, (x + d) % 4, u, c, 1]
        state.setdefault(("sib", u), []).append(send(s, s, sibling))

    def near(u):
        state["pair", u].wait_recv()
        for g in gathers(u)[0]:
            g[0]()

    def far(u):
        near, far = gathers(u)
        for n in range(2):
            near[n][1]()
            far[n][0]()
        for n in range(2):
            to_sibling(u, 0, n)

    def far_mid(u):
        for which, key in enumerate(("fy", "fx")):
            for n, d in ((0, 3), (1, 1)):
                state[key, u][n].wait_recv()
                to_sibling(u, d, which)

    def far_end(u):
        for which, key in enumerate(("fy", "fx")):
            state[key, u][2].wait_recv()
            to_sibling(u, 2, which)

    def up(u):
        once(state["sib", u])
        while weights_in:
            weights_in.pop().wait()
        for which, w in enumerate((wg, wu)):

            @pl.loop(0, 2)
            def _(n):
                lhs = jnp.concatenate(
                    [feats[s // 8, s // 4 % 2, s % 4, u].reshape(ROWS, 128) for s in range(32)], axis=1
                )
                cols = pl.ds(pl.multiple_of(n * 256, 256), 256)
                got = jnp.dot(lhs, w[:, cols], preferred_element_type=F32)
                at = pl.ds(pl.multiple_of(which * 512 + n * 256, 256), 256)
                part[u, :, :, at] = got.reshape(4, QUARTER, 256)

        half = QUARTER // 2
        state["z", u] = ring_scatter(
            ("zs", u), lambda chunk, h: part[u, chunk, h * half : h * half + half, :], zs.at[u], zr.at[u]
        )
        state["z", u][0]()

    def z_on(u):
        state["z", u][1]()

    def h_gather(u):
        half = QUARTER // 2
        return ring_gather(("h", u), lambda m: hid.at[u, m], lambda m, h: hid.at[u, m, pl.ds(h * half, half)])

    def act(u):
        _, _, done, total = state["z", u]
        done()
        half = QUARTER // 2
        for h in range(2):
            both = total(h)
            gate, up = both[:, :512], both[:, 512:]
            value = gate / (1.0 + jnp.exp(-gate)) * up
            hid[u, k, h * half : h * half + half, :] = value.astype(BF16)
        h_gather(u)[0]()

    def h_on(u):
        h_gather(u)[1]()

    def down(i):
        b, p = i // 2, i % 2
        for u in range(b * PER, b * PER + PER):
            once(state["h", u])
        while down_in:
            down_in.pop().wait()

        def tile(half, n):
            cols = pl.ds(pl.multiple_of(half * 2048 + p * 1024 + n * 512, 512), 512)
            got = jnp.dot(hid[b * PER : b * PER + PER].reshape(256, 512), wd[:, cols], preferred_element_type=F32)
            return got.reshape(4, 4, 16, 512)

        @pl.loop(0, 2)
        def _(n):
            xs[i, :, :, :, pl.ds(pl.multiple_of(n * 512, 512), 512)] = tile(1 - c, n).astype(xs.dtype)

        state["swap", i] = send(xs.at[i], xr.at[i], sibling)

        @pl.loop(0, 2)
        def _(n):
            mix[i, :, :, :, pl.ds(pl.multiple_of(n * 512, 512), 512)] = tile(c, n)

    def mixed(i):
        state["swap", i].wait_recv()
        if i % 2 == 0:
            read = lambda m: mix[i, m] + xr[i, m].astype(F32)
        else:
            read = lambda m: mix[i, :, m] + xr[i, :, m].astype(F32)
        state["m1", i] = scatter(("first", i), "yx"[i % 2], read, s1.at[i], r1.at[i])
        state["m1", i][0]()

    def mixed_end(i):
        q1[i] = state["m1", i][1]()
        state["m2", i] = scatter(("second", i), "xy"[i % 2], lambda m: q1[i, m], s2.at[i], r2.at[i])
        state["m2", i][0]()

    def rest_end(i):
        b, p = i // 2, i % 2
        res[b, p] = state["m2", i][1]()
        q = b // 2
        state["rest", q, p] = state.get(("rest", q, p), 0) + 1
        if state["rest", q, p] == 2:
            state["low", q, p] = send(res.at[2 * q + (1 - l), p], pair_in.at[q, p], partner)

    def low(i):
        q, p = i // 2, i % 2
        state["low", q, p].wait_recv()
        fin[q, p] = (res[2 * q + l, p] + pair_in[q, p]).astype(BF16)

    def last(p):
        state["last", p] = send(fin.at[1 - c, p], fin_in.at[p], sibling)
        out_ref[:, pl.ds(pl.multiple_of(c * 2048 + p * 1024, 1024), 1024)] = fin[c, p]

    steps = (pair, near, far, far_mid, far_end, up, z_on, act, h_on, down, mixed, mixed_end, rest_end, low, last)
    for n, i in ORDER:
        steps[n](i)
    for p in range(2):
        state["last", p].wait_recv()
        out_ref[:, pl.ds(pl.multiple_of((1 - c) * 2048 + p * 1024, 1024), 1024)] = fin_in[p]
    for copy in sent:
        copy.wait_send()
    assert len(sent) <= MAX_SEMS


def local(tokens, gate_weight, up_weight, down_weight):
    scratch = [
        pltpu.VMEM((4096, 512), BF16),
        pltpu.VMEM((4096, 512), BF16),
        pltpu.VMEM((512, 4096), BF16),
        pltpu.VMEM((UNITS, 2, 2 * QUARTER, 128), BF16),
        pltpu.VMEM((UNITS, 2 * QUARTER, 128), BF16),
        pltpu.VMEM((4, 2, 4, UNITS, 2, 2, QUARTER, 128), BF16),
        pltpu.VMEM((UNITS, 4, QUARTER, 1024), F32),
        pltpu.VMEM((UNITS, 6, QUARTER // 2, 1024), BF16),
        pltpu.VMEM((UNITS, 6, QUARTER // 2, 1024), BF16),
        pltpu.VMEM((UNITS, 4, QUARTER, 512), BF16),
        pltpu.VMEM((2 * BLOCKS, 4, 4, 16, 1024), BF16),
        pltpu.VMEM((2 * BLOCKS, 4, 4, 16, 1024), BF16),
        pltpu.VMEM((2 * BLOCKS, 4, 4, 16, 1024), F32),
        pltpu.VMEM((2 * BLOCKS, 3, 4, 16, 1024), BF16),
        pltpu.VMEM((2 * BLOCKS, 3, 4, 16, 1024), BF16),
        pltpu.VMEM((2 * BLOCKS, 4, 16, 1024), F32),
        pltpu.VMEM((2 * BLOCKS, 3, 16, 1024), REST),
        pltpu.VMEM((2 * BLOCKS, 3, 16, 1024), REST),
        pltpu.VMEM((BLOCKS, 2, 16, 1024), F32),
        pltpu.VMEM((2, 2, 16, 1024), F32),
        pltpu.VMEM((2, 2, 16, 1024), BF16),
        pltpu.VMEM((2, 16, 1024), BF16),
        pltpu.SemaphoreType.DMA((3,)),
        pltpu.SemaphoreType.DMA((MAX_SEMS,)),
        pltpu.SemaphoreType.DMA((MAX_SEMS,)),
    ]
    return pl.pallas_call(
        kernel,
        name="swiglu_layer",
        out_shape=jax.ShapeDtypeStruct((16, 4096), BF16),
        in_specs=[pl.BlockSpec(memory_space=pltpu.VMEM)] + [pl.BlockSpec(memory_space=pl.ANY)] * 3,
        out_specs=pl.BlockSpec(memory_space=pltpu.VMEM),
        scratch_shapes=scratch,
        cost_estimate=pl.CostEstimate(flops=12_900_000_000, bytes_accessed=13_000_000, transcendentals=131072),
        compiler_params=pltpu.CompilerParams(
            collective_id=0, has_side_effects=True, vmem_limit_bytes=62 * 2**20
        ),
    )(tokens, gate_weight, up_weight, down_weight)


def solution(mesh):
    placed = (P(None, ("gx", "gy")), P("gx", "gy"), P("gx", "gy"), P("gy", "gx"))
    return jax.shard_map(local, mesh=mesh, in_specs=placed, out_specs=P("gy", "gx"), check_vma=False)
```

```python
import functools

import jax
import jax.numpy as jnp
from jax import lax
from jax.experimental import pallas as pl
from jax.experimental.pallas import tpu as pltpu
from jax.sharding import PartitionSpec as P

MESH = pl.DeviceIdType.MESH
F32, BF16 = jnp.float32, jnp.bfloat16
BLOCKS = 4
UNITS = 8
PER = UNITS // BLOCKS
ROWS = 1024 // UNITS
QUARTER = ROWS // 4
REST = F32
MAX_SEMS = 384

ORDER = (
    (0, 0), (0, 4), (0, 3), (0, 1), (0, 7), (1, 0), (1, 3), (1, 1), (1, 4), (2, 0), (2, 1), (0, 6),
    (2, 4), (0, 2), (1, 6), (3, 0), (4, 0), (2, 3), (1, 7), (1, 2), (3, 1), (4, 1), (5, 0), (5, 1),
    (3, 4), (3, 3), (2, 6), (6, 0), (4, 3), (2, 2), (0, 5), (6, 1), (5, 3), (7, 0), (1, 5), (3, 6),
    (7, 1), (3, 2), (4, 2), (4, 6), (6, 3), (4, 4), (2, 7), (5, 2), (5, 4), (3, 7), (2, 5), (6, 2),
    (4, 7), (8, 1), (8, 0), (5, 6), (3, 5), (4, 5), (7, 2), (7, 3), (9, 1), (5, 5), (9, 0), (6, 4),
    (8, 2), (10, 1), (8, 3), (6, 5), (5, 7), (10, 0), (7, 4), (9, 3), (9, 2), (7, 5), (6, 7), (10, 3),
    (11, 1), (6, 6), (8, 4), (10, 2), (8, 5), (7, 7), (11, 0), (7, 6), (9, 5), (11, 3), (8, 7), (9, 4),
    (8, 6), (10, 5), (10, 4), (9, 7), (9, 6), (10, 7), (10, 6), (11, 5), (11, 2), (11, 4), (12, 0), (12, 3),
    (12, 1), (11, 7), (11, 6), (12, 2), (13, 0), (12, 5), (12, 4), (12, 7), (12, 6), (13, 3), (13, 1),
    (13, 2),
)

def kernel(
    tok_ref, wg_hbm, wu_hbm, wd_hbm, out_ref,
    wg, wu, wd, twin, twin_in, feats, part, zs, zr, hid, xs, xr, mix,
    s1, r1, q1, s2, r2, res, ends,
    load_sem, send_sem, recv_sem,
):
    k, j = lax.axis_index("gx"), lax.axis_index("gy")
    c, x, l, y = j % 2, (j // 2) % 4, (j // 8) % 2, j // 16

    def gy(y, l, x, c):
        return ((y * 2 + l) * 4 + x) * 2 + c

    def at_x(d):
        return (k, gy(y, l, (x + d) % 4, c))

    def at_y(d):
        return (k, gy((y + d) % 4, l, x, c))

    def at_k(d):
        return ((k + d) % 4, j)

    sibling = (k, gy(y, l, x, 1 - c))
    partner = (k, gy(y, 1 - l, x, c))
    where = {"x": at_x, "y": at_y, "k": at_k}
    mine = {"x": x, "y": y, "k": k}

    loads = []
    for n, (src, dst) in enumerate(((wg_hbm, wg), (wu_hbm, wu), (wd_hbm, wd))):
        copy = pltpu.make_async_copy(src, dst, load_sem.at[n])
        copy.start()
        loads.append(copy)

    barrier = pltpu.get_barrier_semaphore()
    peers = [sibling, partner, (k, gy(y, 1 - l, x, 1 - c))]
    peers += [at(d) for at in (at_x, at_y) for d in (1, 3, 2)]
    peers += [at_k(1), at_k(3)]
    for peer in peers:
        pl.semaphore_signal(barrier, inc=1, device_id=peer, device_id_type=MESH)

    sent = []

    def send(src, dst, to):
        n = len(sent)
        copy = pltpu.make_async_remote_copy(
            src_ref=src, dst_ref=dst, send_sem=send_sem.at[n], recv_sem=recv_sem.at[n],
            device_id=to, device_id_type=MESH,
        )
        copy.start()
        sent.append(copy.wait_send)
        return copy

    for y_at in range(4):
        for l_at in range(2):
            first = y_at * 256 + l_at * 128
            v = tok_ref[:, first : first + 128].astype(F32)
            v = jnp.concatenate([v, v], axis=0).T.astype(BF16)
            for group in range(8):
                x_at, c_at = group // 2, group % 2
                at = (2 * c_at + l_at) * 256 + y_at * 64 + x_at * 16
                u, row = at // ROWS, at % ROWS
                twin[u, row // (2 * QUARTER), row % (2 * QUARTER) : row % (2 * QUARTER) + 16, :] = (
                    v[group * 16 : group * 16 + 16, :]
                )

    pl.semaphore_wait(barrier, len(peers))
    first_swap = send(twin.at[:, 1 - c], twin_in, sibling)
    state = {}

    def gather(key, axis, own):
        at = where[axis]

        def start():
            s = own(mine[axis])
            state[key] = [send(s, s, at(1)), send(s, s, at(3)), send(s, s, at(2))]

        def done():
            once(state[key])

        return start, done

    def ring_gather(key, own, part_of):
        def start():
            s = own(k)
            state[key] = [send(s, s, at_k(1)), send(s, s, at_k(3))]

        def forward():
            left, right = state[key]
            left.wait_recv()
            s = part_of((k + 3) % 4, 0)
            on = [send(s, s, at_k(1))]
            right.wait_recv()
            s = part_of((k + 1) % 4, 1)
            on.append(send(s, s, at_k(3)))
            state[key] = on

        return start, forward

    def scatter(key, axis, read, st, rc):
        m, at = mine[axis], where[axis]

        def start():
            copies = []
            for n, d in enumerate((2, 1, 3)):
                st[n] = read((m + d) % 4).astype(st.dtype)
                copies.append(send(st.at[n], rc.at[n], at(d)))
            state[key] = copies

        def done():
            value = read(m)
            for n in (1, 2, 0):
                state[key][n].wait_recv()
                value = value + rc[n].astype(F32)
            return value

        return start, done

    def ring_scatter(key, read, st, rc):
        def put(n, value):
            st[n] = value.astype(BF16)

        def start():
            opp, nxt, prv = (k + 2) % 4, (k + 1) % 4, (k + 3) % 4
            put(0, read(opp, 0))
            put(1, read(opp, 1))
            first = [send(st.at[0], rc.at[0], at_k(1)), send(st.at[1], rc.at[1], at_k(3))]
            put(2, read(nxt, 1))
            put(3, read(prv, 0))
            rest = [send(st.at[2], rc.at[2], at_k(1)), send(st.at[3], rc.at[3], at_k(3))]
            state[key] = (first, rest)

        def forward():
            first, rest = state[key]
            first[0].wait_recv()
            put(4, read((k + 1) % 4, 0) + rc[0].astype(F32))
            rest.append(send(st.at[4], rc.at[4], at_k(1)))
            first[1].wait_recv()
            put(5, read((k + 3) % 4, 1) + rc[1].astype(F32))
            rest.append(send(st.at[5], rc.at[5], at_k(3)))

        def done():
            once(state[key][1])

        def total(h):
            value = read(k, h)
            for n in (3, 4) if h == 0 else (2, 5):
                value = value + rc[n].astype(F32)
            return value

        return start, forward, done, total

    def once(copies):
        for copy in copies:
            copy.wait_recv()
        copies.clear()

    swap_in, weights_in, down_in = [first_swap], loads[:2], loads[2:]

    def pair(u):
        once(swap_in)
        own, other = twin[u, c], twin_in[u]
        lane = lax.broadcasted_iota(jnp.int32, own.shape, 1)
        low = jnp.where(lane < 64, 0, 1) == c
        block = jnp.where(low, own.astype(F32), other.astype(F32)).astype(BF16)
        feats[y, l, x, u, c] = block.reshape(2, QUARTER, 128)
        s = feats.at[y, l, x, u, c]
        state["pair", u] = send(s, s, partner)

    def gathers(u):
        near = [
            gather(("nx", u), "x", lambda m: feats.at[y, :, m, u, c, 0]),
            gather(("ny", u), "y", lambda m: feats.at[m, :, x, u, c, 1]),
        ]
        far = [
            gather(("fy", u), "y", lambda m: feats.at[m, :, :, u, c, 0]),
            gather(("fx", u), "x", lambda m: feats.at[:, :, m, u, c, 1]),
        ]
        return near, far

    def to_sibling(u, d, which):
        s = feats.at[(y + d) % 4, :, :, u, c, 0] if which == 0 else feats.at[:, :, (x + d) % 4, u, c, 1]
        state.setdefault(("sib", u), []).append(send(s, s, sibling))

    def near(u):
        state["pair", u].wait_recv()
        for g in gathers(u)[0]:
            g[0]()

    def far(u):
        near, far = gathers(u)
        for n in range(2):
            near[n][1]()
            far[n][0]()
        for n in range(2):
            to_sibling(u, 0, n)

    def far_mid(u):
        for which, key in enumerate(("fy", "fx")):
            for n, d in ((0, 3), (1, 1)):
                state[key, u][n].wait_recv()
                to_sibling(u, d, which)

    def far_end(u):
        for which, key in enumerate(("fy", "fx")):
            state[key, u][2].wait_recv()
            to_sibling(u, 2, which)

    def up(u):
        once(state["sib", u])
        while weights_in:
            weights_in.pop().wait()
        for which, w in enumerate((wg, wu)):

            @pl.loop(0, 2)
            def _(n):
                lhs = jnp.concatenate(
                    [feats[s // 8, s // 4 % 2, s % 4, u].reshape(ROWS, 128) for s in range(32)], axis=1
                )
                cols = pl.ds(pl.multiple_of(n * 256, 256), 256)
                got = jnp.dot(lhs, w[:, cols], preferred_element_type=F32)
                at = pl.ds(pl.multiple_of(which * 512 + n * 256, 256), 256)
                part[u, :, :, at] = got.reshape(4, QUARTER, 256)

        half = QUARTER // 2
        state["z", u] = ring_scatter(
            ("zs", u), lambda chunk, h: part[u, chunk, h * half : h * half + half, :], zs.at[u], zr.at[u]
        )
        state["z", u][0]()

    def z_on(u):
        state["z", u][1]()

    def h_gather(u):
        half = QUARTER // 2
        return ring_gather(("h", u), lambda m: hid.at[u, m], lambda m, h: hid.at[u, m, pl.ds(h * half, half)])

    def act(u):
        _, _, done, total = state["z", u]
        done()
        half = QUARTER // 2
        for h in range(2):
            both = total(h)
            gate, up = both[:, :512], both[:, 512:]
            value = gate / (1.0 + jnp.exp(-gate)) * up
            hid[u, k, h * half : h * half + half, :] = value.astype(BF16)
        h_gather(u)[0]()

    def h_on(u):
        h_gather(u)[1]()

    def down(i):
        b, p = i // 2, i % 2
        for u in range(b * PER, b * PER + PER):
            once(state["h", u])
        while down_in:
            down_in.pop().wait()

        def tile(half, n):
            cols = pl.ds(pl.multiple_of(half * 2048 + p * 1024 + n * 512, 512), 512)
            got = jnp.dot(hid[b * PER : b * PER + PER].reshape(256, 512), wd[:, cols], preferred_element_type=F32)
            return got.reshape(4, 4, 16, 512)

        @pl.loop(0, 2)
        def _(n):
            xs[i, :, :, :, pl.ds(pl.multiple_of(n * 512, 512), 512)] = tile(1 - c, n).astype(xs.dtype)

        state["swap", i] = send(xs.at[i], xr.at[i], sibling)

        @pl.loop(0, 2)
        def _(n):
            mix[i, :, :, :, pl.ds(pl.multiple_of(n * 512, 512), 512)] = tile(c, n)

    def mixed(i):
        state["swap", i].wait_recv()
        if i % 2 == 0:
            read = lambda m: mix[i, m] + xr[i, m].astype(F32)
        else:
            read = lambda m: mix[i, :, m] + xr[i, :, m].astype(F32)
        state["m1", i] = scatter(("first", i), "yx"[i % 2], read, s1.at[i], r1.at[i])
        state["m1", i][0]()

    def mixed_end(i):
        q1[i] = state["m1", i][1]()
        state["m2", i] = scatter(("second", i), "xy"[i % 2], lambda m: q1[i, m], s2.at[i], r2.at[i])
        state["m2", i][0]()

    def rest_end(i):
        b, p = i // 2, i % 2
        res[b, p] = state["m2", i][1]()
        q = b // 2
        state["rest", q, p] = state.get(("rest", q, p), 0) + 1
        if state["rest", q, p] == 2:
            to_owner(q, p)

    def to_owner(q, p):
        n = len(sent)

        def copy(src, slot, send_at, to):
            return pltpu.make_async_remote_copy(
                src_ref=src, dst_ref=ends.at[q, p, slot], send_sem=send_sem.at[send_at],
                recv_sem=recv_sem.at[n + slot], device_id=to, device_id_type=MESH,
            )

        across = copy(res.at[2 * q + (1 - l), p], c, n, (k, gy(y, 1 - l, x, q)))
        beside = copy(res.at[2 * q + l, p], 2, n + 1, sibling)
        across.start()

        @pl.when(c != q)
        def _():
            beside.start()

        def sent_beside():
            @pl.when(c != q)
            def _():
                beside.wait_send()

        sent.extend((across.wait_send, sent_beside, lambda: None))
        state["low", q, p] = [copy(res.at[2 * q + l, p], slot, n, sibling) for slot in range(3)]

    def low(i):
        q, p = i // 2, i % 2

        @pl.when(c == q)
        def _():
            for copy in state["low", q, p]:
                copy.wait_recv()
            own, other = res[2 * q + l, p] + ends[q, p, q], ends[q, p, 2] + ends[q, p, 1 - q]
            out_ref[:, q * 2048 + p * 1024 : q * 2048 + p * 1024 + 1024] = own.astype(BF16)
            at = (1 - q) * 2048 + p * 1024
            out_ref[:, at : at + 1024] = other.astype(BF16)

    steps = (pair, near, far, far_mid, far_end, up, z_on, act, h_on, down, mixed, mixed_end, rest_end, low)
    settled = 0
    for place, (n, i) in enumerate(ORDER):
        if place >= len(ORDER) - 12:
            until = min(settled + 40, len(sent) - 12)
            for wait_send in sent[settled:until]:
                wait_send()
            settled = max(settled, until)
        steps[n](i)
    for wait_send in sent[settled:]:
        wait_send()
    assert len(sent) <= MAX_SEMS


def local(tokens, gate_weight, up_weight, down_weight):
    scratch = [
        pltpu.VMEM((4096, 512), BF16),
        pltpu.VMEM((4096, 512), BF16),
        pltpu.VMEM((512, 4096), BF16),
        pltpu.VMEM((UNITS, 2, 2 * QUARTER, 128), BF16),
        pltpu.VMEM((UNITS, 2 * QUARTER, 128), BF16),
        pltpu.VMEM((4, 2, 4, UNITS, 2, 2, QUARTER, 128), BF16),
        pltpu.VMEM((UNITS, 4, QUARTER, 1024), F32),
        pltpu.VMEM((UNITS, 6, QUARTER // 2, 1024), BF16),
        pltpu.VMEM((UNITS, 6, QUARTER // 2, 1024), BF16),
        pltpu.VMEM((UNITS, 4, QUARTER, 512), BF16),
        pltpu.VMEM((2 * BLOCKS, 4, 4, 16, 1024), BF16),
        pltpu.VMEM((2 * BLOCKS, 4, 4, 16, 1024), BF16),
        pltpu.VMEM((2 * BLOCKS, 4, 4, 16, 1024), F32),
        pltpu.VMEM((2 * BLOCKS, 3, 4, 16, 1024), BF16),
        pltpu.VMEM((2 * BLOCKS, 3, 4, 16, 1024), BF16),
        pltpu.VMEM((2 * BLOCKS, 4, 16, 1024), F32),
        pltpu.VMEM((2 * BLOCKS, 3, 16, 1024), REST),
        pltpu.VMEM((2 * BLOCKS, 3, 16, 1024), REST),
        pltpu.VMEM((BLOCKS, 2, 16, 1024), F32),
        pltpu.VMEM((2, 2, 3, 16, 1024), F32),
        pltpu.SemaphoreType.DMA((3,)),
        pltpu.SemaphoreType.DMA((MAX_SEMS,)),
        pltpu.SemaphoreType.DMA((MAX_SEMS,)),
    ]
    return pl.pallas_call(
        kernel,
        name="swiglu_layer",
        out_shape=jax.ShapeDtypeStruct((16, 4096), BF16),
        in_specs=[pl.BlockSpec(memory_space=pltpu.VMEM)] + [pl.BlockSpec(memory_space=pl.ANY)] * 3,
        out_specs=pl.BlockSpec(memory_space=pltpu.VMEM),
        scratch_shapes=scratch,
        cost_estimate=pl.CostEstimate(flops=12_900_000_000, bytes_accessed=13_000_000, transcendentals=131072),
        compiler_params=pltpu.CompilerParams(
            collective_id=0, has_side_effects=True, vmem_limit_bytes=62 * 2**20
        ),
    )(tokens.T, gate_weight, up_weight, down_weight)


def solution(mesh):
    placed = (P(None, ("gx", "gy")), P("gx", "gy"), P("gx", "gy"), P("gy", "gx"))
    return jax.shard_map(local, mesh=mesh, in_specs=placed, out_specs=P("gy", "gx"), check_vma=False)
```

```python
import functools

import jax
import jax.numpy as jnp
from jax import lax
from jax.experimental import pallas as pl
from jax.experimental.pallas import tpu as pltpu
from jax.sharding import PartitionSpec as P

MESH = pl.DeviceIdType.MESH
F32, BF16 = jnp.float32, jnp.bfloat16
BLOCKS = 4
UNITS = 8
PER = UNITS // BLOCKS
ROWS = 1024 // UNITS
QUARTER = ROWS // 4
REST = F32
MAX_SEMS = 384

ORDER = (
    (0, 6), (0, 2), (0, 7), (0, 3), (0, 1), (0, 0), (1, 6), (1, 2), (1, 3), (1, 1), (2, 6), (0, 4),
    (2, 2), (1, 7), (2, 3), (1, 0), (3, 6), (4, 6), (2, 1), (3, 2), (5, 6), (4, 2), (0, 5), (1, 4),
    (5, 2), (3, 3), (4, 3), (6, 6), (2, 7), (2, 0), (5, 3), (3, 7), (2, 4), (6, 2), (7, 6), (4, 7),
    (6, 3), (5, 7), (3, 1), (7, 2), (1, 5), (4, 1), (5, 1), (2, 5), (3, 0), (4, 0), (7, 3), (6, 7),
    (5, 0), (8, 3), (8, 2), (3, 5), (6, 1), (7, 7), (4, 5), (8, 6), (5, 5), (3, 4), (4, 4), (9, 3),
    (9, 2), (8, 7), (6, 0), (5, 4), (10, 2), (7, 1), (10, 3), (9, 6), (7, 0), (9, 7), (6, 5), (10, 6),
    (6, 4), (10, 7), (8, 1), (8, 0), (7, 5), (11, 3), (7, 4), (11, 2), (9, 1), (9, 0), (11, 6), (8, 4),
    (11, 7), (8, 5), (10, 0), (10, 1), (9, 5), (9, 4), (12, 6), (10, 5), (10, 4), (11, 0), (12, 3), (11, 1),
    (11, 4), (12, 7), (12, 2), (11, 5), (12, 0), (12, 1), (12, 4), (12, 5), (13, 2), (13, 1), (13, 0), (13, 3),
)

def kernel(
    tok_ref, wg_hbm, wu_hbm, wd_hbm, out_ref,
    wg, wu, wd, twin, twin_in, feats, part, zs, zr, hid, xs, xr, mix,
    s1, r1, q1, s2, r2, res, ends,
    load_sem, send_sem, recv_sem,
):
    k, j = lax.axis_index("gx"), lax.axis_index("gy")
    c, x, l, y = j % 2, (j // 2) % 4, (j // 8) % 2, j // 16

    def gy(y, l, x, c):
        return ((y * 2 + l) * 4 + x) * 2 + c

    def at_x(d):
        return (k, gy(y, l, (x + d) % 4, c))

    def at_y(d):
        return (k, gy((y + d) % 4, l, x, c))

    def at_k(d):
        return ((k + d) % 4, j)

    sibling = (k, gy(y, l, x, 1 - c))
    partner = (k, gy(y, 1 - l, x, c))
    where = {"x": at_x, "y": at_y, "k": at_k}
    mine = {"x": x, "y": y, "k": k}

    loads = []
    for n, (src, dst) in enumerate(((wg_hbm, wg), (wu_hbm, wu), (wd_hbm, wd))):
        copy = pltpu.make_async_copy(src, dst, load_sem.at[n])
        copy.start()
        loads.append(copy)

    barrier = pltpu.get_barrier_semaphore()
    peers = [sibling, partner, (k, gy(y, 1 - l, x, 1 - c))]
    peers += [at(d) for at in (at_x, at_y) for d in (1, 3, 2)]
    peers += [at_k(1), at_k(3)]
    for peer in peers:
        pl.semaphore_signal(barrier, inc=1, device_id=peer, device_id_type=MESH)

    sent = []

    def send(src, dst, to):
        n = len(sent)
        copy = pltpu.make_async_remote_copy(
            src_ref=src, dst_ref=dst, send_sem=send_sem.at[n], recv_sem=recv_sem.at[n],
            device_id=to, device_id_type=MESH,
        )
        copy.start()
        sent.append(copy.wait_send)
        return copy

    for y_at in range(4):
        for l_at in range(2):
            first = y_at * 256 + l_at * 128
            v = tok_ref[:, first : first + 128].astype(F32)
            v = jnp.concatenate([v, v], axis=0).T.astype(BF16)
            for group in range(8):
                x_at, c_at = group // 2, group % 2
                at = (2 * c_at + l_at) * 256 + y_at * 64 + x_at * 16
                u, row = at // ROWS, at % ROWS
                twin[u, row // (2 * QUARTER), row % (2 * QUARTER) : row % (2 * QUARTER) + 16, :] = (
                    v[group * 16 : group * 16 + 16, :]
                )

    pl.semaphore_wait(barrier, len(peers))
    first_swap = send(twin.at[:, 1 - c], twin_in, sibling)
    state = {}

    def gather(key, axis, own):
        at = where[axis]

        def start():
            s = own(mine[axis])
            state[key] = [send(s, s, at(1)), send(s, s, at(3)), send(s, s, at(2))]

        def done():
            once(state[key])

        return start, done

    def ring_gather(key, own, part_of):
        def start():
            s = own(k)
            state[key] = [send(s, s, at_k(1)), send(s, s, at_k(3))]

        def forward():
            left, right = state[key]
            left.wait_recv()
            s = part_of((k + 3) % 4, 0)
            on = [send(s, s, at_k(1))]
            right.wait_recv()
            s = part_of((k + 1) % 4, 1)
            on.append(send(s, s, at_k(3)))
            state[key] = on

        return start, forward

    def scatter(key, axis, read, st, rc):
        m, at = mine[axis], where[axis]

        def start():
            copies = []
            for n, d in enumerate((2, 1, 3)):
                st[n] = read((m + d) % 4).astype(st.dtype)
                copies.append(send(st.at[n], rc.at[n], at(d)))
            state[key] = copies

        def done():
            value = read(m)
            for n in (1, 2, 0):
                state[key][n].wait_recv()
                value = value + rc[n].astype(F32)
            return value

        return start, done

    def ring_scatter(key, read, st, rc):
        def put(n, value):
            st[n] = value.astype(BF16)

        def start():
            opp, nxt, prv = (k + 2) % 4, (k + 1) % 4, (k + 3) % 4
            put(0, read(opp, 0))
            put(1, read(opp, 1))
            first = [send(st.at[0], rc.at[0], at_k(1)), send(st.at[1], rc.at[1], at_k(3))]
            put(2, read(nxt, 1))
            put(3, read(prv, 0))
            rest = [send(st.at[2], rc.at[2], at_k(1)), send(st.at[3], rc.at[3], at_k(3))]
            state[key] = (first, rest)

        def forward():
            first, rest = state[key]
            first[0].wait_recv()
            put(4, read((k + 1) % 4, 0) + rc[0].astype(F32))
            rest.append(send(st.at[4], rc.at[4], at_k(1)))
            first[1].wait_recv()
            put(5, read((k + 3) % 4, 1) + rc[1].astype(F32))
            rest.append(send(st.at[5], rc.at[5], at_k(3)))

        def done():
            once(state[key][1])

        def total(h):
            value = read(k, h)
            for n in (3, 4) if h == 0 else (2, 5):
                value = value + rc[n].astype(F32)
            return value

        return start, forward, done, total

    def once(copies):
        for copy in copies:
            copy.wait_recv()
        copies.clear()

    swap_in, weights_in, down_in = [first_swap], loads[:2], loads[2:]

    def pair(u):
        once(swap_in)
        own, other = twin[u, c], twin_in[u]
        lane = lax.broadcasted_iota(jnp.int32, own.shape, 1)
        low = jnp.where(lane < 64, 0, 1) == c
        block = jnp.where(low, own.astype(F32), other.astype(F32)).astype(BF16)
        feats[y, l, x, u, c] = block.reshape(2, QUARTER, 128)
        s = feats.at[y, l, x, u, c]
        state["pair", u] = send(s, s, partner)

    def gathers(u):
        near = [
            gather(("nx", u), "x", lambda m: feats.at[y, :, m, u, c, 0]),
            gather(("ny", u), "y", lambda m: feats.at[m, :, x, u, c, 1]),
        ]
        far = [
            gather(("fy", u), "y", lambda m: feats.at[m, :, :, u, c, 0]),
            gather(("fx", u), "x", lambda m: feats.at[:, :, m, u, c, 1]),
        ]
        return near, far

    def to_sibling(u, d, which):
        s = feats.at[(y + d) % 4, :, :, u, c, 0] if which == 0 else feats.at[:, :, (x + d) % 4, u, c, 1]
        state.setdefault(("sib", u), []).append(send(s, s, sibling))

    def near(u):
        state["pair", u].wait_recv()
        for g in gathers(u)[0]:
            g[0]()

    def far(u):
        near, far = gathers(u)
        for n in range(2):
            near[n][1]()
            far[n][0]()
        for n in range(2):
            to_sibling(u, 0, n)

    def far_mid(u):
        for which, key in enumerate(("fy", "fx")):
            for n, d in ((0, 3), (1, 1)):
                state[key, u][n].wait_recv()
                to_sibling(u, d, which)

    def far_end(u):
        for which, key in enumerate(("fy", "fx")):
            state[key, u][2].wait_recv()
            to_sibling(u, 2, which)

    def up(u):
        once(state["sib", u])
        while weights_in:
            weights_in.pop().wait()
        for which, w in enumerate((wg, wu)):

            @pl.loop(0, 2)
            def _(n):
                lhs = jnp.concatenate(
                    [feats[s // 8, s // 4 % 2, s % 4, u].reshape(ROWS, 128) for s in range(32)], axis=1
                )
                cols = pl.ds(pl.multiple_of(n * 256, 256), 256)
                got = jnp.dot(lhs, w[:, cols], preferred_element_type=F32)
                at = pl.ds(pl.multiple_of(which * 512 + n * 256, 256), 256)
                part[u, :, :, at] = got.reshape(4, QUARTER, 256)

        half = QUARTER // 2
        state["z", u] = ring_scatter(
            ("zs", u), lambda chunk, h: part[u, chunk, h * half : h * half + half, :], zs.at[u], zr.at[u]
        )
        state["z", u][0]()

    def z_on(u):
        state["z", u][1]()

    def h_gather(u):
        half = QUARTER // 2
        return ring_gather(("h", u), lambda m: hid.at[u, m], lambda m, h: hid.at[u, m, pl.ds(h * half, half)])

    def act(u):
        _, _, done, total = state["z", u]
        done()
        half = QUARTER // 2
        for h in range(2):
            both = total(h)
            gate, up = both[:, :512], both[:, 512:]
            value = gate / (1.0 + jnp.exp(-gate)) * up
            hid[u, k, h * half : h * half + half, :] = value.astype(BF16)
        h_gather(u)[0]()

    def h_on(u):
        h_gather(u)[1]()

    def down(i):
        b, p = i // 2, i % 2
        for u in range(b * PER, b * PER + PER):
            once(state["h", u])
        while down_in:
            down_in.pop().wait()

        def tile(half, n):
            cols = pl.ds(pl.multiple_of(half * 2048 + p * 1024 + n * 512, 512), 512)
            got = jnp.dot(hid[b * PER : b * PER + PER].reshape(256, 512), wd[:, cols], preferred_element_type=F32)
            return got.reshape(4, 4, 16, 512)

        @pl.loop(0, 2)
        def _(n):
            xs[i, :, :, :, pl.ds(pl.multiple_of(n * 512, 512), 512)] = tile(1 - c, n).astype(xs.dtype)

        state["swap", i] = send(xs.at[i], xr.at[i], sibling)

        @pl.loop(0, 2)
        def _(n):
            mix[i, :, :, :, pl.ds(pl.multiple_of(n * 512, 512), 512)] = tile(c, n)

    def mixed(i):
        state["swap", i].wait_recv()
        if i % 2 == 0:
            read = lambda m: mix[i, m] + xr[i, m].astype(F32)
        else:
            read = lambda m: mix[i, :, m] + xr[i, :, m].astype(F32)
        state["m1", i] = scatter(("first", i), "yx"[i % 2], read, s1.at[i], r1.at[i])
        state["m1", i][0]()

    def mixed_end(i):
        q1[i] = state["m1", i][1]()
        state["m2", i] = scatter(("second", i), "xy"[i % 2], lambda m: q1[i, m], s2.at[i], r2.at[i])
        state["m2", i][0]()

    def rest_end(i):
        b, p = i // 2, i % 2
        res[b, p] = state["m2", i][1]()
        q = b // 2
        state["rest", q, p] = state.get(("rest", q, p), 0) + 1
        if state["rest", q, p] == 2:
            to_owner(q, p)

    def to_owner(q, p):
        n = len(sent)

        def copy(src, slot, send_at, to):
            return pltpu.make_async_remote_copy(
                src_ref=src, dst_ref=ends.at[q, p, slot], send_sem=send_sem.at[send_at],
                recv_sem=recv_sem.at[n + slot], device_id=to, device_id_type=MESH,
            )

        across = copy(res.at[2 * q + (1 - l), p], c, n, (k, gy(y, 1 - l, x, q)))
        beside = copy(res.at[2 * q + l, p], 2, n + 1, sibling)
        across.start()

        @pl.when(c != q)
        def _():
            beside.start()

        def sent_beside():
            @pl.when(c != q)
            def _():
                beside.wait_send()

        sent.extend((across.wait_send, sent_beside, lambda: None))
        state["low", q, p] = [copy(res.at[2 * q + l, p], slot, n, sibling) for slot in range(3)]

    def low(i):
        q, p = i // 2, i % 2

        @pl.when(c == q)
        def _():
            for copy in state["low", q, p]:
                copy.wait_recv()
            own, other = res[2 * q + l, p] + ends[q, p, q], ends[q, p, 2] + ends[q, p, 1 - q]
            out_ref[:, q * 2048 + p * 1024 : q * 2048 + p * 1024 + 1024] = own.astype(BF16)
            at = (1 - q) * 2048 + p * 1024
            out_ref[:, at : at + 1024] = other.astype(BF16)

    steps = (pair, near, far, far_mid, far_end, up, z_on, act, h_on, down, mixed, mixed_end, rest_end, low)
    settled = 0
    for place, (n, i) in enumerate(ORDER):
        if place >= len(ORDER) - 12:
            until = min(settled + 40, len(sent) - 12)
            for wait_send in sent[settled:until]:
                wait_send()
            settled = max(settled, until)
        steps[n](i)
    for wait_send in sent[settled:]:
        wait_send()
    assert len(sent) <= MAX_SEMS


def local(tokens, gate_weight, up_weight, down_weight):
    scratch = [
        pltpu.VMEM((4096, 512), BF16),
        pltpu.VMEM((4096, 512), BF16),
        pltpu.VMEM((512, 4096), BF16),
        pltpu.VMEM((UNITS, 2, 2 * QUARTER, 128), BF16),
        pltpu.VMEM((UNITS, 2 * QUARTER, 128), BF16),
        pltpu.VMEM((4, 2, 4, UNITS, 2, 2, QUARTER, 128), BF16),
        pltpu.VMEM((UNITS, 4, QUARTER, 1024), F32),
        pltpu.VMEM((UNITS, 6, QUARTER // 2, 1024), BF16),
        pltpu.VMEM((UNITS, 6, QUARTER // 2, 1024), BF16),
        pltpu.VMEM((UNITS, 4, QUARTER, 512), BF16),
        pltpu.VMEM((2 * BLOCKS, 4, 4, 16, 1024), BF16),
        pltpu.VMEM((2 * BLOCKS, 4, 4, 16, 1024), BF16),
        pltpu.VMEM((2 * BLOCKS, 4, 4, 16, 1024), F32),
        pltpu.VMEM((2 * BLOCKS, 3, 4, 16, 1024), BF16),
        pltpu.VMEM((2 * BLOCKS, 3, 4, 16, 1024), BF16),
        pltpu.VMEM((2 * BLOCKS, 4, 16, 1024), F32),
        pltpu.VMEM((2 * BLOCKS, 3, 16, 1024), REST),
        pltpu.VMEM((2 * BLOCKS, 3, 16, 1024), REST),
        pltpu.VMEM((BLOCKS, 2, 16, 1024), F32),
        pltpu.VMEM((2, 2, 3, 16, 1024), F32),
        pltpu.SemaphoreType.DMA((3,)),
        pltpu.SemaphoreType.DMA((MAX_SEMS,)),
        pltpu.SemaphoreType.DMA((MAX_SEMS,)),
    ]
    return pl.pallas_call(
        kernel,
        name="swiglu_layer",
        out_shape=jax.ShapeDtypeStruct((16, 4096), BF16),
        in_specs=[pl.BlockSpec(memory_space=pltpu.VMEM)] + [pl.BlockSpec(memory_space=pl.ANY)] * 3,
        out_specs=pl.BlockSpec(memory_space=pltpu.VMEM),
        scratch_shapes=scratch,
        cost_estimate=pl.CostEstimate(flops=12_900_000_000, bytes_accessed=13_000_000, transcendentals=131072),
        compiler_params=pltpu.CompilerParams(
            collective_id=0, has_side_effects=True, vmem_limit_bytes=62 * 2**20
        ),
    )(tokens.T, gate_weight, up_weight, down_weight)


def solution(mesh):
    placed = (P(None, ("gx", "gy")), P("gx", "gy"), P("gx", "gy"), P("gy", "gx"))
    return jax.shard_map(local, mesh=mesh, in_specs=placed, out_specs=P("gy", "gx"), check_vma=False)
```

```python
import functools

import jax
import jax.numpy as jnp
from jax import lax
from jax.experimental import pallas as pl
from jax.experimental.pallas import tpu as pltpu
from jax.sharding import PartitionSpec as P

MESH = pl.DeviceIdType.MESH
F32, BF16 = jnp.float32, jnp.bfloat16
BLOCKS = 4
UNITS = 8
PER = UNITS // BLOCKS
ROWS = 1024 // UNITS
QUARTER = ROWS // 4
REST = F32
MAX_SEMS = 384

ORDER = (
    (0, 6), (0, 2), (0, 7), (0, 3), (0, 1), (0, 0), (1, 6), (1, 2), (1, 3), (1, 1), (2, 6), (0, 4),
    (2, 2), (1, 7), (2, 3), (1, 0), (3, 6), (4, 6), (2, 1), (3, 2), (5, 6), (4, 2), (0, 5), (1, 4),
    (5, 2), (3, 3), (4, 3), (6, 6), (2, 7), (2, 0), (5, 3), (3, 7), (2, 4), (6, 2), (7, 6), (4, 7),
    (6, 3), (5, 7), (3, 1), (7, 2), (1, 5), (4, 1), (5, 1), (2, 5), (3, 0), (4, 0), (7, 3), (6, 7),
    (5, 0), (8, 3), (8, 2), (3, 5), (6, 1), (7, 7), (4, 5), (8, 6), (5, 5), (3, 4), (4, 4), (9, 3),
    (9, 2), (8, 7), (6, 0), (5, 4), (10, 2), (7, 1), (10, 3), (9, 6), (7, 0), (9, 7), (6, 5), (10, 6),
    (6, 4), (10, 7), (8, 1), (8, 0), (7, 5), (11, 3), (7, 4), (11, 2), (9, 1), (9, 0), (11, 6), (8, 4),
    (11, 7), (8, 5), (10, 0), (10, 1), (9, 5), (9, 4), (12, 6), (10, 5), (10, 4), (11, 0), (12, 3), (11, 1),
    (11, 4), (12, 7), (12, 2), (11, 5), (12, 0), (12, 1), (12, 4), (12, 5), (13, 2), (13, 1), (13, 0), (13, 3),
)

def kernel(
    tok_ref, wg_hbm, wu_hbm, wd_hbm, out_ref,
    wg, wu, wd, twin, twin_in, feats, part, zs, zr, hid, xs, xr, mix,
    s1, r1, q1, s2, r2, res, ends,
    load_sem, send_sem, recv_sem,
):
    k, j = lax.axis_index("gx"), lax.axis_index("gy")
    c, x, l, y = j % 2, (j // 2) % 4, (j // 8) % 2, j // 16

    def gy(y, l, x, c):
        return ((y * 2 + l) * 4 + x) * 2 + c

    def at_x(d):
        return (k, gy(y, l, (x + d) % 4, c))

    def at_y(d):
        return (k, gy((y + d) % 4, l, x, c))

    def at_k(d):
        return ((k + d) % 4, j)

    sibling = (k, gy(y, l, x, 1 - c))
    partner = (k, gy(y, 1 - l, x, c))
    where = {"x": at_x, "y": at_y, "k": at_k}
    mine = {"x": x, "y": y, "k": k}

    barrier = pltpu.get_barrier_semaphore()
    peers = [sibling, partner, (k, gy(y, 1 - l, x, 1 - c))]
    peers += [at(d) for at in (at_x, at_y) for d in (1, 3, 2)]
    peers += [at_k(1), at_k(3)]
    for peer in peers:
        pl.semaphore_signal(barrier, inc=1, device_id=peer, device_id_type=MESH)

    loads = []
    for n, (src, dst) in enumerate(((wg_hbm, wg), (wu_hbm, wu), (wd_hbm, wd))):
        copy = pltpu.make_async_copy(src, dst, load_sem.at[n])
        copy.start()
        loads.append(copy)

    sent = []

    def send(src, dst, to):
        n = len(sent)
        copy = pltpu.make_async_remote_copy(
            src_ref=src, dst_ref=dst, send_sem=send_sem.at[n], recv_sem=recv_sem.at[n],
            device_id=to, device_id_type=MESH,
        )
        copy.start()
        sent.append(copy.wait_send)
        return copy

    for y_at in range(4):
        for l_at in range(2):
            first = y_at * 256 + l_at * 128
            v = tok_ref[:, first : first + 128].astype(F32)
            v = jnp.concatenate([v, v], axis=0).T.astype(BF16)
            for group in range(8):
                x_at, c_at = group // 2, group % 2
                at = (2 * c_at + l_at) * 256 + y_at * 64 + x_at * 16
                u, row = at // ROWS, at % ROWS
                twin[u, row // (2 * QUARTER), row % (2 * QUARTER) : row % (2 * QUARTER) + 16, :] = (
                    v[group * 16 : group * 16 + 16, :]
                )

    pl.semaphore_wait(barrier, len(peers))
    first_swap = send(twin.at[:, 1 - c], twin_in, sibling)
    state = {}

    def gather(key, axis, own):
        at = where[axis]

        def start():
            s = own(mine[axis])
            state[key] = [send(s, s, at(1)), send(s, s, at(3)), send(s, s, at(2))]

        def done():
            once(state[key])

        return start, done

    def ring_gather(key, own, part_of):
        def start():
            s = own(k)
            state[key] = [send(s, s, at_k(1)), send(s, s, at_k(3))]

        def forward():
            left, right = state[key]
            left.wait_recv()
            s = part_of((k + 3) % 4, 0)
            on = [send(s, s, at_k(1))]
            right.wait_recv()
            s = part_of((k + 1) % 4, 1)
            on.append(send(s, s, at_k(3)))
            state[key] = on

        return start, forward

    def scatter(key, axis, read, st, rc):
        m, at = mine[axis], where[axis]

        def start():
            copies = []
            for n, d in enumerate((2, 1, 3)):
                st[n] = read((m + d) % 4).astype(st.dtype)
                copies.append(send(st.at[n], rc.at[n], at(d)))
            state[key] = copies

        def done():
            value = read(m)
            for n in (1, 2, 0):
                state[key][n].wait_recv()
                value = value + rc[n].astype(F32)
            return value

        return start, done

    def ring_scatter(key, read, st, rc):
        def put(n, value):
            st[n] = value.astype(BF16)

        def start():
            opp, nxt, prv = (k + 2) % 4, (k + 1) % 4, (k + 3) % 4
            put(0, read(opp, 0))
            put(1, read(opp, 1))
            first = [send(st.at[0], rc.at[0], at_k(1)), send(st.at[1], rc.at[1], at_k(3))]
            put(2, read(nxt, 1))
            put(3, read(prv, 0))
            rest = [send(st.at[2], rc.at[2], at_k(1)), send(st.at[3], rc.at[3], at_k(3))]
            state[key] = (first, rest)

        def forward():
            first, rest = state[key]
            first[0].wait_recv()
            put(4, read((k + 1) % 4, 0) + rc[0].astype(F32))
            rest.append(send(st.at[4], rc.at[4], at_k(1)))
            first[1].wait_recv()
            put(5, read((k + 3) % 4, 1) + rc[1].astype(F32))
            rest.append(send(st.at[5], rc.at[5], at_k(3)))

        def done():
            once(state[key][1])

        def total(h):
            value = read(k, h)
            for n in (3, 4) if h == 0 else (2, 5):
                value = value + rc[n].astype(F32)
            return value

        return start, forward, done, total

    def once(copies):
        for copy in copies:
            copy.wait_recv()
        copies.clear()

    swap_in, weights_in, down_in = [first_swap], loads[:2], loads[2:]

    def pair(u):
        once(swap_in)
        own, other = twin[u, c], twin_in[u]
        lane = lax.broadcasted_iota(jnp.int32, own.shape, 1)
        low = jnp.where(lane < 64, 0, 1) == c
        block = jnp.where(low, own.astype(F32), other.astype(F32)).astype(BF16)
        feats[y, l, x, u, c] = block.reshape(2, QUARTER, 128)
        s = feats.at[y, l, x, u, c]
        state["pair", u] = send(s, s, partner)

    def gathers(u):
        near = [
            gather(("nx", u), "x", lambda m: feats.at[y, :, m, u, c, 0]),
            gather(("ny", u), "y", lambda m: feats.at[m, :, x, u, c, 1]),
        ]
        far = [
            gather(("fy", u), "y", lambda m: feats.at[m, :, :, u, c, 0]),
            gather(("fx", u), "x", lambda m: feats.at[:, :, m, u, c, 1]),
        ]
        return near, far

    def to_sibling(u, d, which):
        s = feats.at[(y + d) % 4, :, :, u, c, 0] if which == 0 else feats.at[:, :, (x + d) % 4, u, c, 1]
        state.setdefault(("sib", u), []).append(send(s, s, sibling))

    def near(u):
        state["pair", u].wait_recv()
        for g in gathers(u)[0]:
            g[0]()

    def far(u):
        near, far = gathers(u)
        for n in range(2):
            near[n][1]()
            far[n][0]()
        for n in range(2):
            to_sibling(u, 0, n)

    def far_mid(u):
        for which, key in enumerate(("fy", "fx")):
            for n, d in ((0, 3), (1, 1)):
                state[key, u][n].wait_recv()
                to_sibling(u, d, which)

    def far_end(u):
        for which, key in enumerate(("fy", "fx")):
            state[key, u][2].wait_recv()
            to_sibling(u, 2, which)

    def up(u):
        once(state["sib", u])
        while weights_in:
            weights_in.pop().wait()
        for which, w in enumerate((wg, wu)):

            @pl.loop(0, 2)
            def _(n):
                lhs = jnp.concatenate(
                    [feats[s // 8, s // 4 % 2, s % 4, u].reshape(ROWS, 128) for s in range(32)], axis=1
                )
                cols = pl.ds(pl.multiple_of(n * 256, 256), 256)
                got = jnp.dot(lhs, w[:, cols], preferred_element_type=F32)
                at = pl.ds(pl.multiple_of(which * 512 + n * 256, 256), 256)
                part[u, :, :, at] = got.reshape(4, QUARTER, 256)

        half = QUARTER // 2
        state["z", u] = ring_scatter(
            ("zs", u), lambda chunk, h: part[u, chunk, h * half : h * half + half, :], zs.at[u], zr.at[u]
        )
        state["z", u][0]()

    def z_on(u):
        state["z", u][1]()

    def h_gather(u):
        half = QUARTER // 2
        return ring_gather(("h", u), lambda m: hid.at[u, m], lambda m, h: hid.at[u, m, pl.ds(h * half, half)])

    def act(u):
        _, _, done, total = state["z", u]
        done()
        half = QUARTER // 2
        for h in range(2):
            both = total(h)
            gate, up = both[:, :512], both[:, 512:]
            value = gate / (1.0 + jnp.exp(-gate)) * up
            hid[u, k, h * half : h * half + half, :] = value.astype(BF16)
        h_gather(u)[0]()

    def h_on(u):
        h_gather(u)[1]()

    def down(i):
        b, p = i // 2, i % 2
        for u in range(b * PER, b * PER + PER):
            once(state["h", u])
        while down_in:
            down_in.pop().wait()

        def tile(half, n):
            cols = pl.ds(pl.multiple_of(half * 2048 + p * 1024 + n * 512, 512), 512)
            got = jnp.dot(hid[b * PER : b * PER + PER].reshape(256, 512), wd[:, cols], preferred_element_type=F32)
            return got.reshape(4, 4, 16, 512)

        state["swap", i] = []
        for n in range(2):
            at = (i, slice(None), slice(None), slice(None), slice(n * 512, n * 512 + 512))
            xs[at] = tile(1 - c, n).astype(xs.dtype)
            state["swap", i].append(send(xs.at[at], xr.at[at], sibling))

        @pl.loop(0, 2)
        def _(n):
            mix[i, :, :, :, pl.ds(pl.multiple_of(n * 512, 512), 512)] = tile(c, n)

    def mixed(i):
        once(state["swap", i])
        if i % 2 == 0:
            read = lambda m: mix[i, m] + xr[i, m].astype(F32)
        else:
            read = lambda m: mix[i, :, m] + xr[i, :, m].astype(F32)
        state["m1", i] = scatter(("first", i), "yx"[i % 2], read, s1.at[i], r1.at[i])
        state["m1", i][0]()

    def mixed_end(i):
        q1[i] = state["m1", i][1]()
        state["m2", i] = scatter(("second", i), "xy"[i % 2], lambda m: q1[i, m], s2.at[i], r2.at[i])
        state["m2", i][0]()

    def rest_end(i):
        b, p = i // 2, i % 2
        res[b, p] = state["m2", i][1]()
        q = b // 2
        state["rest", q, p] = state.get(("rest", q, p), 0) + 1
        if state["rest", q, p] == 2:
            to_owner(q, p)

    def to_owner(q, p):
        n = len(sent)

        def copy(src, slot, send_at, to):
            return pltpu.make_async_remote_copy(
                src_ref=src, dst_ref=ends.at[q, p, slot], send_sem=send_sem.at[send_at],
                recv_sem=recv_sem.at[n + slot], device_id=to, device_id_type=MESH,
            )

        across = copy(res.at[2 * q + (1 - l), p], c, n, (k, gy(y, 1 - l, x, q)))
        beside = copy(res.at[2 * q + l, p], 2, n + 1, sibling)
        across.start()

        @pl.when(c != q)
        def _():
            beside.start()

        def sent_beside():
            @pl.when(c != q)
            def _():
                beside.wait_send()

        sent.extend((across.wait_send, sent_beside, lambda: None))
        state["low", q, p] = [copy(res.at[2 * q + l, p], slot, n, sibling) for slot in range(3)]

    def low(i):
        q, p = i // 2, i % 2

        @pl.when(c == q)
        def _():
            for copy in state["low", q, p]:
                copy.wait_recv()
            own, other = res[2 * q + l, p] + ends[q, p, q], ends[q, p, 2] + ends[q, p, 1 - q]
            out_ref[:, q * 2048 + p * 1024 : q * 2048 + p * 1024 + 1024] = own.astype(BF16)
            at = (1 - q) * 2048 + p * 1024
            out_ref[:, at : at + 1024] = other.astype(BF16)

    steps = (pair, near, far, far_mid, far_end, up, z_on, act, h_on, down, mixed, mixed_end, rest_end, low)
    settled = 0
    for place, (n, i) in enumerate(ORDER):
        if place >= len(ORDER) - 20:
            until = min(settled + 40, len(sent) - 12)
            for wait_send in sent[settled:until]:
                wait_send()
            settled = max(settled, until)
        steps[n](i)
    for wait_send in sent[settled:]:
        wait_send()
    assert len(sent) <= MAX_SEMS


def local(tokens, gate_weight, up_weight, down_weight):
    scratch = [
        pltpu.VMEM((4096, 512), BF16),
        pltpu.VMEM((4096, 512), BF16),
        pltpu.VMEM((512, 4096), BF16),
        pltpu.VMEM((UNITS, 2, 2 * QUARTER, 128), BF16),
        pltpu.VMEM((UNITS, 2 * QUARTER, 128), BF16),
        pltpu.VMEM((4, 2, 4, UNITS, 2, 2, QUARTER, 128), BF16),
        pltpu.VMEM((UNITS, 4, QUARTER, 1024), F32),
        pltpu.VMEM((UNITS, 6, QUARTER // 2, 1024), BF16),
        pltpu.VMEM((UNITS, 6, QUARTER // 2, 1024), BF16),
        pltpu.VMEM((UNITS, 4, QUARTER, 512), BF16),
        pltpu.VMEM((2 * BLOCKS, 4, 4, 16, 1024), BF16),
        pltpu.VMEM((2 * BLOCKS, 4, 4, 16, 1024), BF16),
        pltpu.VMEM((2 * BLOCKS, 4, 4, 16, 1024), F32),
        pltpu.VMEM((2 * BLOCKS, 3, 4, 16, 1024), BF16),
        pltpu.VMEM((2 * BLOCKS, 3, 4, 16, 1024), BF16),
        pltpu.VMEM((2 * BLOCKS, 4, 16, 1024), F32),
        pltpu.VMEM((2 * BLOCKS, 3, 16, 1024), REST),
        pltpu.VMEM((2 * BLOCKS, 3, 16, 1024), REST),
        pltpu.VMEM((BLOCKS, 2, 16, 1024), F32),
        pltpu.VMEM((2, 2, 3, 16, 1024), F32),
        pltpu.SemaphoreType.DMA((3,)),
        pltpu.SemaphoreType.DMA((MAX_SEMS,)),
        pltpu.SemaphoreType.DMA((MAX_SEMS,)),
    ]
    return pl.pallas_call(
        kernel,
        name="swiglu_layer",
        out_shape=jax.ShapeDtypeStruct((16, 4096), BF16),
        in_specs=[pl.BlockSpec(memory_space=pltpu.VMEM)] + [pl.BlockSpec(memory_space=pl.ANY)] * 3,
        out_specs=pl.BlockSpec(memory_space=pltpu.VMEM),
        scratch_shapes=scratch,
        cost_estimate=pl.CostEstimate(flops=12_900_000_000, bytes_accessed=13_000_000, transcendentals=131072),
        compiler_params=pltpu.CompilerParams(
            collective_id=0, has_side_effects=True, vmem_limit_bytes=62 * 2**20
        ),
    )(tokens.T, gate_weight, up_weight, down_weight)


def solution(mesh):
    placed = (P(None, ("gx", "gy")), P("gx", "gy"), P("gx", "gy"), P("gy", "gx"))
    return jax.shard_map(local, mesh=mesh, in_specs=placed, out_specs=P("gy", "gx"), check_vma=False)
```
